32 devices in a mesh: gx: 4 (over x, core), gy: 8 (over z, y).
Axes of the slice: x: 2, y: 2, z: 4, core: 2. Of those that a mesh axis runs over, the one named last changes fastest.
Arguments:
- nest_state: float32 [4, 8, 96, 3072], P(None, None, 'gx', 'gy'), may hold values from -6 to 6
- parent_state: float32 [4, 8, 96, 3072], P(None, None, 'gx', 'gy'), may hold values from -6 to 6
- offset_x: int32 [1], replicated, may hold values from 1 to 15
- offset_y: int32 [1], replicated, may hold values from 385 to 511
Outputs:
- nest_out: float32 [4, 8, 96, 3072], P(None, None, 'gx', 'gy')
- parent_out: float32 [4, 8, 96, 3072], P(None, None, 'gx', 'gy')
The draws below stay inside these ranges and needn't reach their ends.
All inputs are finite; a program needn't handle non-finite values.
Results may differ from the reference program's by a relative error of at most 0.00019.
Values sent between devices are 32-bit elements; how exact they have to be, the bound alone decides.
A program may use at most 128 MiB of HBM per device.

```python
import jax
import jax.numpy as jnp
from jax import lax

LV = 8
SUBSTEPS = 3
CPX = 24
CPY = 384
NXN = 96
NYN = 3072
NXP = 96
NYP = 3072
N_GX = 4
N_GY = 8


def block_scale(rng, dims, shards, smallest, largest):
    def one(position, blocks):
        draws = jax.random.uniform(jax.random.fold_in(jax.random.fold_in(rng, 6), position), (blocks,), jnp.float32, smallest / len(shards), largest / len(shards))
        return jnp.repeat(jnp.exp(draws), dims[position] // blocks).reshape((-1,) + (1,) * (len(dims) - position - 1))

    level = one(*shards[0])
    for cut in shards[1:]:
        level = level * one(*cut)
    return level


def bell_draw(key, extent, deviation, bound, pieces=(), held_as=jnp.bfloat16):
    level = block_scale(key, extent, pieces, -0.22, 0.18) if pieces else 1.0
    result = jax.random.normal(key, extent, jnp.float32) * deviation * level
    return jnp.minimum(jnp.maximum(result, -bound), bound).astype(held_as)


def setup_inputs(seed: int = 0) -> dict:
    key_list = jax.random.split(jax.random.key(seed), 5)
    return {
        "nest_state": bell_draw(key_list[0], (4, LV, NXN, NYN), 1.0, 6.0, ((2, 4), (3, 8)), jnp.float32),
        "parent_state": bell_draw(key_list[1], (4, LV, NXP, NYP), 1.0, 6.0, ((2, 4), (3, 8)), jnp.float32),
        "offset_x": jax.random.randint(key_list[2], (1,), max(1, (N_GX // 2 - 1) * CPX - NXN // 3), max(max(1, (N_GX // 2 - 1) * CPX - NXN // 3) + 1, min(NXP - NXN // 3, (N_GX // 2) * CPX - NXN // 3))).astype(jnp.int32),
        "offset_y": jax.random.randint(key_list[3], (1,), max(CPY + 1, (N_GY // 2 - 1) * CPY - NYN // 3), max(max(CPY + 1, (N_GY // 2 - 1) * CPY - NYN // 3) + 1, min(NYP - NYN // 3, (N_GY // 2) * CPY - NYN // 3))).astype(jnp.int32),
    }


CARRY_RATE = 0.35
SOUND_RATE = 0.4
MIXING_RATE = 0.2


def advance(padded):
    center = padded[:, :, 1:-1, 1:-1]
    slope_x = (padded[:, :, 2:, 1:-1] - padded[:, :, :-2, 1:-1]) * 0.5
    slope_y = (padded[:, :, 1:-1, 2:] - padded[:, :, 1:-1, :-2]) * 0.5
    carried = center[0][None] * slope_x[:3] + center[1][None] * slope_y[:3]
    potential = center[2]
    level_above = jnp.concatenate([potential[1:], potential[-1:]], axis=0)
    level_below = jnp.concatenate([potential[:1], potential[:-1]], axis=0)
    wind_east = center[0] - CARRY_RATE * carried[0] - SOUND_RATE * slope_x[3]
    wind_north = center[1] - CARRY_RATE * carried[1] - SOUND_RATE * slope_y[3]
    heat_next = potential - CARRY_RATE * carried[2] + MIXING_RATE * (level_above - 2.0 * potential + level_below)
    pressure = center[3] - SOUND_RATE * (slope_x[0] + slope_y[1])
    return jnp.stack([wind_east, wind_north, heat_next, pressure])


def reference(nest_state, parent_state, offset_x, offset_y):
    shift_x = offset_x[0].astype(jnp.int32)
    shift_y = offset_y[0].astype(jnp.int32)
    zero_index = jnp.zeros((), jnp.int32)
    span_x = NXN // 3
    span_y = NYN // 3
    west = lax.dynamic_slice(parent_state, (zero_index, zero_index, shift_x - 1, shift_y), (4, LV, 1, span_y))
    east = lax.dynamic_slice(parent_state, (zero_index, zero_index, shift_x + span_x, shift_y), (4, LV, 1, span_y))
    south = lax.dynamic_slice(parent_state, (zero_index, zero_index, shift_x, shift_y - 1), (4, LV, span_x, 1))
    north = lax.dynamic_slice(parent_state, (zero_index, zero_index, shift_x, shift_y + span_y), (4, LV, span_x, 1))
    frame = jnp.zeros((4, LV, NXN + 2, NYN + 2), jnp.float32)
    frame = frame.at[:, :, 0:1, 1:-1].set(jnp.repeat(west, 3, axis=3))
    frame = frame.at[:, :, -1:, 1:-1].set(jnp.repeat(east, 3, axis=3))
    frame = frame.at[:, :, 1:-1, 0:1].set(jnp.repeat(south, 3, axis=2))
    frame = frame.at[:, :, 1:-1, -1:].set(jnp.repeat(north, 3, axis=2))
    fields = nest_state
    for substep in range(SUBSTEPS):
        fields = advance(frame.at[:, :, 1:-1, 1:-1].set(fields))
    parent_next = advance(jnp.pad(parent_state, ((0, 0), (0, 0), (1, 1), (1, 1))))
    coarse = fields[:3].reshape(3, LV, span_x, 3, span_y, 3).mean(axis=(3, 5))
    parent_out = lax.dynamic_update_slice(parent_next, coarse, (zero_index, zero_index, shift_x, shift_y))
    return fields, parent_out
```

```python
import functools

import jax
import jax.numpy as jnp
from jax import lax
from jax.experimental import pallas as pl
from jax.experimental.pallas import tpu as pltpu
from jax.sharding import PartitionSpec as P

SUBSTEPS = 3
CARRY_RATE = 0.35
SOUND_RATE = 0.4
MIXING_RATE = 0.2
MESH = pl.DeviceIdType.MESH
F32 = jnp.float32


def quotient(a, b):
    return a // b if isinstance(a, int) else lax.div(a, jnp.int32(b))


class Line:
    def __init__(self, count, parent, nest, lowest):
        self.count, self.parent, self.nest = count, parent, nest
        self.coarse = nest // 3
        span = count * self.coarse
        self.span = span
        self.low = max(lowest, (count // 2 - 1) * parent - span)
        self.high = max(self.low, min(count * parent - span, (count // 2) * parent - span) - 1)
        self.lift = self.high // self.coarse + 2
        tiles = range(count)
        self.slots = max(self.last(i) - self.first(i) + 1 for i in tiles)
        hit = [(t, i) for i in tiles for t in range(self.first(i), self.last(i) + 1)]
        assert all(0 <= t < count for t, _ in hit)
        self.sources = max(i - self.base(t) + 1 for t, i in hit)
        assert min(i - self.base(t) for t, i in hit) >= 0
        reach = max(parent * t - self.coarse * self.base(t) - self.low for t, _ in hit) + parent
        self.window = max(self.sources, -(-reach // self.coarse)) * self.coarse
        self.tile_low, self.tile_high = self.first(0), self.last(count - 1)
        self.before = ((self.low - 1) // parent, (self.high - 1) // parent)
        self.after = ((self.low + span) // parent, (self.high + span) // parent)
        assert self.before[1] < self.after[0]

    def first(self, i):
        return quotient(self.low + self.coarse * i - 1, self.parent)

    def last(self, i):
        return quotient(self.high + self.coarse * i + self.coarse, self.parent)

    def base(self, t):
        return quotient(self.parent * t - self.high - 1 + self.lift * self.coarse, self.coarse) - self.lift


def kernel(lx, ly, levels, off_x, off_y, nest, parent, nest_out, parent_out,
           fa, fb, pp, xs, xr, ys, yr, cs, cr, rs, rr, gx, gy, coarse, back,
           s_halo, r_halo, s_col, r_col, s_row, r_row, s_back, r_back):
    ix, iy = lax.axis_index("gx"), lax.axis_index("gy")
    ox, oy = off_x[0], off_y[0]
    cols, rows = lx.nest, ly.nest
    wide, high = fa.shape[3], fa.shape[2]
    fields = levels * 4
    n_before = lx.before[1] - lx.before[0] + 1
    n_after = lx.after[1] - lx.after[0] + 1
    n_col = max(n_before, n_after)

    def there(tx, ty):
        return {"gx": tx, "gy": ty}

    def send(ok, src, dst, ssem, rsem, tx, ty, local=True):
        mine = (tx == ix) & (ty == iy)

        @pl.when(ok & jnp.logical_not(mine))
        def _():
            pltpu.make_async_remote_copy(src, dst, ssem, rsem, device_id=there(tx, ty), device_id_type=MESH).start()

        if local:
            @pl.when(ok & mine)
            def _():
                pltpu.make_async_copy(src, dst, rsem).start()

    def sent(ok, src, ssem, tx, ty):
        @pl.when(ok & jnp.logical_not((tx == ix) & (ty == iy)))
        def _():
            pltpu.make_async_copy(src, src, ssem).wait()

    def arrived(ok, dst, rsem, blank=True):
        @pl.when(ok)
        def _():
            pltpu.make_async_copy(dst, dst, rsem).wait()

        if blank:
            @pl.when(jnp.logical_not(ok))
            def _():
                dst[...] = jnp.zeros(dst.shape, F32)

    lane = lax.broadcasted_iota(jnp.int32, (1, 128), 1)

    in_rows = (iy >= ly.tile_low) & (iy <= ly.tile_high)
    in_cols = (ix >= lx.tile_low) & (ix <= lx.tile_high)
    gives_west = (ix >= lx.before[0]) & (ix <= lx.before[1])
    gives_east = (ix >= lx.after[0]) & (ix <= lx.after[1])
    gives_col = in_rows & (gives_west | gives_east)
    col_to = jnp.where(gives_west, 0, lx.count - 1)
    col_slot = ix - jnp.where(gives_west, lx.before[0], lx.after[0])
    gives_south = iy == ly.before[0]
    gives_north = iy == ly.after[0]
    gives_row = in_cols & (gives_south | gives_north)
    row_to = jnp.where(gives_south, 0, ly.count - 1)

    @pl.when(gives_col)
    def _():
        want = ox + jnp.where(gives_west, -1, lx.span) - lx.parent * ix
        sub = lax.broadcasted_iota(jnp.int32, (lx.parent, ly.parent), 0)
        hit = sub == want

        def body(k, _):
            for c in range(4):
                line = jnp.sum(jnp.where(hit, parent[c, k], 0.0), axis=0, keepdims=True)
                cs[pl.ds(c * levels + k, 1), :] = line
            return 0

        lax.fori_loop(0, levels, body, 0)

    def col_targets():
        for j in range(ly.sources):
            ty = ly.base(iy) + j
            tyc = jnp.clip(ty, 0, ly.count - 1)
            ok = gives_col & (ty >= 0) & (ty < ly.count) & (iy >= ly.first(tyc)) & (iy <= ly.last(tyc))
            yield ok, j, tyc, jnp.clip(iy - ly.first(tyc), 0, ly.slots - 1)

    for ok, j, ty, part in col_targets():
        slot = jnp.clip(col_slot, 0, n_col - 1)
        send(ok, cs, cr.at[slot, part], s_col.at[j], r_col.at[slot, part], col_to, ty)

    @pl.when(gives_row)
    def _():
        want = oy + jnp.where(gives_south, -1, ly.span) - ly.parent * iy
        hit = lax.broadcasted_iota(jnp.int32, (lx.parent, ly.parent), 1) == want

        def body(k, acc):
            for c in range(4):
                line = jnp.sum(jnp.where(hit, parent[c, k], 0.0), axis=1, keepdims=True)
                acc = jnp.where(lane == c * levels + k, line, acc)
            return acc

        rs[...] = lax.fori_loop(0, levels, body, jnp.zeros((lx.parent, 128), F32))

    def row_targets():
        for j in range(lx.sources):
            tx = lx.base(ix) + j
            txc = jnp.clip(tx, 0, lx.count - 1)
            ok = gives_row & (tx >= 0) & (tx < lx.count) & (ix >= lx.first(txc)) & (ix <= lx.last(txc))
            yield ok, j, txc, jnp.clip(ix - lx.first(txc), 0, lx.slots - 1)

    for ok, j, tx, part in row_targets():
        send(ok, rs, rr.at[part], s_row.at[j], r_row.at[part], tx, row_to)

    half = levels // 2

    def pack_x(k, _):
        for c in range(4):
            for part in range(2):
                lev = k + part * half
                r = 4 * part
                xs[0, c, k, r:r + 3, :] = nest[c, lev, 0:3, :]
                xs[0, c, k, r + 3:r + 4, :] = parent[c, lev, 0:1, :]
                xs[1, c, k, r:r + 3, :] = nest[c, lev, cols - 3:cols, :]
                xs[1, c, k, r + 3:r + 4, :] = parent[c, lev, cols - 1:cols, :]
        return 0

    lax.fori_loop(0, half, pack_x, 0)

    has = {-1: lambda i, n: i > 0, 0: lambda i, n: i >= 0, 1: lambda i, n: i < n - 1}

    def neighbour(dx, dy):
        ok = has[dx](ix, lx.count) & has[dy](iy, ly.count)
        return ok, jnp.clip(ix + dx, 0, lx.count - 1), jnp.clip(iy + dy, 0, ly.count - 1)

    def halo_sends():
        for n, (dx, dy) in enumerate([(-1, 0), (1, 0), (0, -1), (0, 1), (-1, -1), (-1, 1), (1, -1), (1, 1)]):
            ok, tx, ty = neighbour(dx, dy)
            if dy == 0:
                src, dst = xs.at[(dx + 1) // 2], xr.at[(dx + 1) // 2]
            else:
                d = (dy + 1) // 2
                if dx == 0:
                    src, dst = ys.at[d], yr.at[d, pl.ds(0, cols)]
                elif dx < 0:
                    src, dst = ys.at[d, pl.ds(0, 8)], yr.at[d, pl.ds(cols, 8)]
                else:
                    src, dst = ys.at[d, pl.ds(cols - 8, 8)], yr.at[d, pl.ds(cols + 8, 8)]
            yield n, dx, dy, ok, tx, ty, src, dst

    for n, dx, dy, ok, tx, ty, src, dst in halo_sends():
        if dy == 0:
            send(ok, src, dst, s_halo.at[n], r_halo.at[n], tx, ty, local=False)

    def pack_y(k, acc):
        low, top = acc
        for c in range(4):
            at = 4 * (c * levels + k)
            mine = (lane >= at) & (lane < at + 4)
            a = jnp.where(lane < 3, nest[c, k, :, 0:128], pltpu.roll(parent[c, k, :, 0:128], 3, 1))
            b = jnp.where(lane < 3, pltpu.roll(nest[c, k, :, rows - 128:rows], 3, 1),
                          pltpu.roll(parent[c, k, :, rows - 128:rows], 4, 1))
            low = jnp.where(mine, pltpu.roll(a, at, 1), low)
            top = jnp.where(mine, pltpu.roll(b, at, 1), top)
        return low, top

    blank = jnp.zeros((cols, 128), F32)
    low, top = lax.fori_loop(0, levels, pack_y, (blank, blank))
    ys[0] = low
    ys[1] = top
    for n, dx, dy, ok, tx, ty, src, dst in halo_sends():
        if dy != 0:
            send(ok, src, dst, s_halo.at[n], r_halo.at[n], tx, ty, local=False)

    def middle(k, _):
        for c in range(4):
            fa[c, k, 0:cols, 0:rows] = nest[c, k]
            pp[c, k, 0:cols, 0:rows] = parent[c, k]
        return 0

    lax.fori_loop(0, levels, middle, 0)

    west, east = ix == 0, ix == lx.count - 1
    south, north = iy == 0, iy == ly.count - 1
    takes_col = west | east
    takes_row = south | north
    for s in range(n_col):
        live = (west & (s < n_before)) | (east & (s < n_after))
        for part in range(ly.slots):
            arrived(live & (ly.first(iy) + part <= ly.last(iy)), cr.at[s, part], r_col.at[s, part])
    for part in range(lx.slots):
        arrived(takes_row & (lx.first(ix) + part <= lx.last(ix)), rr.at[part], r_row.at[part])

    def third(v):
        return (((v + 3) * 21846) >> 16) - 1

    @pl.when(takes_col)
    def _():
        y = lax.broadcasted_iota(jnp.int32, (1, wide), 1)
        y = jnp.where(y < rows + 64, y, y - wide)
        place = oy + ly.coarse * iy - ly.parent * ly.first(iy) + third(y)
        total = jnp.zeros((fields, wide), F32)
        for part in range(ly.slots):
            k = lax.broadcasted_iota(jnp.int32, (ly.parent, wide), 0) + part * ly.parent
            table = jnp.where(k == place, 1.0, 0.0).astype(F32)
            strip = cr[0, part]
            for s in range(1, n_col):
                strip = strip + cr[s, part]
            total = total + jnp.dot(strip, table, precision=lax.Precision.HIGHEST, preferred_element_type=F32)
        gx[...] = total

    @pl.when(takes_row)
    def _():
        total = jnp.zeros((high, 128), F32)
        x = lax.broadcasted_iota(jnp.int32, (high, 1), 0)
        x = jnp.where(x < cols + 4, x, x - high)
        place = ox + lx.coarse * ix - lx.parent * lx.first(ix) + third(x)
        for part in range(lx.slots):
            k = lax.broadcasted_iota(jnp.int32, (high, lx.parent), 1) + part * lx.parent
            table = jnp.where(k == place, 1.0, 0.0).astype(F32)
            total = total + jnp.dot(table, rr[part], precision=lax.Precision.HIGHEST, preferred_element_type=F32)

        def body(k, _):
            for c in range(4):
                turned = pltpu.roll(total, lax.rem(128 - (c * levels + k), 128), 1)
                gy[c, k] = jnp.broadcast_to(turned[:, 0:1], (high, 128))
            return 0

        lax.fori_loop(0, levels, body, 0)

    sub8 = lax.broadcasted_iota(jnp.int32, (8, 1), 0)
    at_x = (sub8 == jnp.where(west, 7, -1)) | (sub8 == jnp.where(east, 0, -1))
    at_y = (lane == jnp.where(south, 127, -1)) | (lane == jnp.where(north, 0, -1))

    def put(dst, c, k, value):
        edge = jnp.where(at_x, gx[pl.ds(c * levels + k, 1), :], value[cols:high, :])
        dst[c, k, 0:cols, 0:rows] = value[0:cols, 0:rows]
        dst[c, k, cols:high, 0:rows] = edge[:, 0:rows]
        dst[c, k, 0:cols, rows:wide] = jnp.where(at_y, gy[c, k, 0:cols, :], value[0:cols, rows:wide])
        dst[c, k, cols:high, rows:wide] = jnp.where(at_y, gy[c, k, cols:high, :], edge[:, rows:wide])

    for n, dx, dy, ok, tx, ty, src, dst in halo_sends():
        back_ok, _, _ = neighbour(-dx, -dy)
        arrived(back_ok, dst, r_halo.at[n])

    def unpack(k, _):
        for c in range(4):
            for part in range(2):
                lev = k + part * half
                r = 4 * part
                fa[c, lev, cols:cols + 3, 0:rows] = xr[0, c, k, r:r + 3, :]
                pp[c, lev, cols:cols + 1, 0:rows] = xr[0, c, k, r + 3:r + 4, :]
                fa[c, lev, high - 3:high, 0:rows] = xr[1, c, k, r:r + 3, :]
                pp[c, lev, high - 1:high, 0:rows] = xr[1, c, k, r + 3:r + 4, :]
        return 0

    lax.fori_loop(0, half, unpack, 0)

    def side(d):
        corner = jnp.where(sub8 < 4, yr[d, cols:cols + 8, :], yr[d, cols + 8:cols + 16, :])
        return jnp.concatenate([yr[d, 0:cols, :], corner], axis=0)

    def unpack_y(k, both):
        after, before = both
        for c in range(4):
            at = 4 * (c * levels + k)
            a = pltpu.roll(after, lax.rem(128 - at, 128), 1)
            b = pltpu.roll(before, lax.rem(253 - at, 128), 1)
            block = jnp.where(lane < 64, a, b)
            fa[c, k, :, rows:wide] = jnp.where(at_y, gy[c, k], block)
            pp[c, k, :, rows:wide] = jnp.where(lane < 64, pltpu.roll(a, 125, 1), pltpu.roll(b, 127, 1))
            fa[c, k, cols:high, :] = jnp.where(at_x, gx[pl.ds(c * levels + k, 1), :], fa[c, k, cols:high, :])
        return both

    lax.fori_loop(0, levels, unpack_y, (side(0), side(1)))

    def advanced(src, k):
        u, v, t, p = (src[c, k] for c in range(4))
        above = src[2, jnp.minimum(k + 1, levels - 1)]
        below = src[2, jnp.maximum(k - 1, 0)]

        def dx(f):
            return pltpu.roll(f, high - 1, 0) - pltpu.roll(f, 1, 0)

        def dy(f):
            return pltpu.roll(f, wide - 1, 1) - pltpu.roll(f, 1, 1)

        ux, vy = dx(u), dy(v)
        hu, hv = u * (CARRY_RATE * 0.5), v * (CARRY_RATE * 0.5)
        s = SOUND_RATE * 0.5
        yield u - (hu * ux + hv * dy(u)) - s * dx(p)
        yield v - (hu * dx(v) + hv * vy) - s * dy(p)
        yield t - (hu * dx(t) + hv * dy(t)) + MIXING_RATE * (above - 2.0 * t + below)
        yield p - s * (ux + vy)

    for src, dst in ((fa, fb), (fb, fa)):
        def step(k, _, src=src, dst=dst):
            for c, value in enumerate(advanced(src, k)):
                put(dst, c, k, value)
            return 0

        lax.fori_loop(0, levels, step, 0)

    k = lax.broadcasted_iota(jnp.int32, (rows, ly.coarse), 0)
    j = lax.broadcasted_iota(jnp.int32, (rows, ly.coarse), 1)
    thirds = jnp.where((k >= 3 * j) & (k < 3 * j + 3), 1.0, 0.0).astype(F32)

    j = lax.broadcasted_iota(jnp.int32, (3 * lx.coarse, 3 * cols), 0)
    k = lax.broadcasted_iota(jnp.int32, (3 * lx.coarse, 3 * cols), 1)
    triples = jnp.where((k >= 3 * j) & (k < 3 * j + 3), 1.0, 0.0).astype(F32)

    def last_step(k, _):
        inner = [value[0:cols, 0:rows] for value in advanced(fa, k)]
        for c in range(4):
            nest_out[c, k] = inner[c]
        sums = jnp.dot(jnp.concatenate(inner[:3], axis=0), thirds, precision=lax.Precision.HIGHEST,
                       preferred_element_type=F32)
        mean = jnp.dot(triples, sums, precision=lax.Precision.HIGHEST, preferred_element_type=F32) * (1.0 / 9.0)
        for c in range(3):
            coarse[c * levels + k] = mean[c * lx.coarse:(c + 1) * lx.coarse, :]
        return 0

    lax.fori_loop(0, levels, last_step, 0)

    def back_targets():
        for a in range(lx.slots):
            for b in range(ly.slots):
                tx, ty = lx.first(ix) + a, ly.first(iy) + b
                ok = (tx <= lx.last(ix)) & (ty <= ly.last(iy))
                tx, ty = jnp.minimum(tx, lx.last(ix)), jnp.minimum(ty, ly.last(iy))
                yield ok, a, b, tx, ty, ix - lx.base(tx), iy - ly.base(ty)

    for ok, a, b, tx, ty, sx, sy in back_targets():
        send(ok, coarse, back.at[sx, sy], s_back.at[a, b], r_back.at[sx, sy], tx, ty)

    def parent_step(k, _):
        for c, value in enumerate(advanced(pp, k)):
            parent_out[c, k] = value[0:lx.parent, 0:ly.parent]
        return 0

    lax.fori_loop(0, levels, parent_step, 0)

    takes_back = in_rows & in_cols
    for a in range(lx.sources):
        for b in range(ly.sources):
            sx, sy = lx.base(ix) + a, ly.base(iy) + b
            sxc, syc = jnp.clip(sx, 0, lx.count - 1), jnp.clip(sy, 0, ly.count - 1)
            ok = takes_back & (sx == sxc) & (sy == syc)
            ok = ok & (ix >= lx.first(sxc)) & (ix <= lx.last(sxc)) & (iy >= ly.first(syc)) & (iy <= ly.last(syc))
            arrived(ok, back.at[a, b], r_back.at[a, b], blank=False)

    @pl.when(takes_back)
    def _():
        col = lax.broadcasted_iota(jnp.int32, (lx.parent, ly.parent), 0) + lx.parent * ix - ox
        row = lax.broadcasted_iota(jnp.int32, (lx.parent, ly.parent), 1) + ly.parent * iy - oy
        inside = (col >= 0) & (col < lx.span) & (row >= 0) & (row < ly.span)
        x0 = lx.parent * ix - lx.coarse * lx.base(ix) - ox
        y0 = ly.parent * iy - ly.coarse * ly.base(iy) - oy
        total = lx.window
        nsy = ly.window // ly.coarse

        def body(k, _):
            for c in range(3):
                f = c * levels + k
                whole = jnp.concatenate(
                    [jnp.concatenate([back[a, b, f] for b in range(nsy)], axis=1) for a in range(total // lx.coarse)],
                    axis=0)
                moved = pltpu.roll(pltpu.roll(whole, total - x0, 0), nsy * ly.coarse - y0, 1)
                parent_out[c, k] = jnp.where(inside, moved[0:lx.parent, 0:ly.parent], parent_out[c, k])
            return 0

        lax.fori_loop(0, levels, body, 0)

    for ok, j, ty, part in col_targets():
        sent(ok, cs, s_col.at[j], col_to, ty)
    for ok, j, tx, part in row_targets():
        sent(ok, rs, s_row.at[j], tx, row_to)
    for n, dx, dy, ok, tx, ty, src, dst in halo_sends():
        sent(ok, src, s_halo.at[n], tx, ty)
    for ok, a, b, tx, ty, sx, sy in back_targets():
        sent(ok, coarse, s_back.at[a, b], tx, ty)


def on_device(lx, ly, nest_state, parent_state, offset_x, offset_y):
    levels = nest_state.shape[1]
    cols, rows = nest_state.shape[2:]
    high, wide = cols + 8, rows + 128
    n_col = max(lx.before[1] - lx.before[0], lx.after[1] - lx.after[0]) + 1
    padded = pltpu.VMEM((4, levels, high, wide), F32)
    dma = pltpu.SemaphoreType.DMA
    nbx, nby = lx.window // lx.coarse, ly.window // ly.coarse
    vm = pl.BlockSpec(memory_space=pltpu.VMEM)
    sm = pl.BlockSpec(memory_space=pltpu.SMEM)
    shape = jax.ShapeDtypeStruct(nest_state.shape, F32)
    return pl.pallas_call(
        functools.partial(kernel, lx, ly, levels),
        out_shape=(shape, shape),
        in_specs=[sm, sm, vm, vm],
        out_specs=(vm, vm),
        scratch_shapes=[
            padded, padded, padded,
            pltpu.VMEM((2, 4, levels // 2, 8, rows), F32),
            pltpu.VMEM((2, 4, levels // 2, 8, rows), F32),
            pltpu.VMEM((2, cols, 128), F32),
            pltpu.VMEM((2, cols + 16, 128), F32),
            pltpu.VMEM((4 * levels, ly.parent), F32),
            pltpu.VMEM((n_col, ly.slots, 4 * levels, ly.parent), F32),
            pltpu.VMEM((lx.parent, 128), F32),
            pltpu.VMEM((lx.slots, lx.parent, 128), F32),
            pltpu.VMEM((4 * levels, wide), F32),
            pltpu.VMEM((4, levels, high, 128), F32),
            pltpu.VMEM((3 * levels, lx.coarse, ly.coarse), F32),
            pltpu.VMEM((nbx, nby, 3 * levels, lx.coarse, ly.coarse), F32),
            dma((8,)), dma((8,)),
            dma((ly.sources,)), dma((n_col, ly.slots)),
            dma((lx.sources,)), dma((lx.slots,)),
            dma((lx.slots, ly.slots)), dma((nbx, nby)),
        ],
        compiler_params=pltpu.CompilerParams(has_side_effects=True, vmem_limit_bytes=48 * 1024 * 1024),
    )(offset_x, offset_y, nest_state, parent_state)


def solution(mesh):
    placed = (P(None, None, "gx", "gy"), P(None, None, "gx", "gy"), P(), P())
    count_x, count_y = mesh.shape["gx"], mesh.shape["gy"]

    def program(nest_state, parent_state, offset_x, offset_y):
        lx = Line(count_x, parent_state.shape[2] // count_x, nest_state.shape[2] // count_x, 1)
        rows = parent_state.shape[3] // count_y
        ly = Line(count_y, rows, nest_state.shape[3] // count_y, rows + 1)
        return jax.shard_map(
            functools.partial(on_device, lx, ly),
            mesh=mesh,
            in_specs=placed,
            out_specs=(P(None, None, "gx", "gy"), P(None, None, "gx", "gy")),
            check_vma=False,
        )(nest_state, parent_state, offset_x, offset_y)

    return program
```

```python
import functools

import jax
import jax.numpy as jnp
from jax import lax
from jax.experimental import pallas as pl
from jax.experimental.pallas import tpu as pltpu
from jax.sharding import PartitionSpec as P

SUBSTEPS = 3
CARRY_RATE = 0.35
SOUND_RATE = 0.4
MIXING_RATE = 0.2
MESH = pl.DeviceIdType.MESH
F32 = jnp.float32


def quotient(a, b):
    return a // b if isinstance(a, int) else lax.div(a, jnp.int32(b))


class Line:
    def __init__(self, count, parent, nest, lowest):
        self.count, self.parent, self.nest = count, parent, nest
        self.coarse = nest // 3
        span = count * self.coarse
        self.span = span
        self.low = max(lowest, (count // 2 - 1) * parent - span)
        self.high = max(self.low, min(count * parent - span, (count // 2) * parent - span) - 1)
        self.lift = self.high // self.coarse + 2
        tiles = range(count)
        self.slots = max(self.last(i) - self.first(i) + 1 for i in tiles)
        hit = [(t, i) for i in tiles for t in range(self.first(i), self.last(i) + 1)]
        assert all(0 <= t < count for t, _ in hit)
        self.sources = max(i - self.base(t) + 1 for t, i in hit)
        assert min(i - self.base(t) for t, i in hit) >= 0
        reach = max(parent * t - self.coarse * self.base(t) - self.low for t, _ in hit) + parent
        self.window = max(self.sources, -(-reach // self.coarse)) * self.coarse
        self.tile_low, self.tile_high = self.first(0), self.last(count - 1)
        self.before = ((self.low - 1) // parent, (self.high - 1) // parent)
        self.after = ((self.low + span) // parent, (self.high + span) // parent)
        assert self.before[1] < self.after[0]

    def first(self, i):
        return quotient(self.low + self.coarse * i - 1, self.parent)

    def last(self, i):
        return quotient(self.high + self.coarse * i + self.coarse, self.parent)

    def base(self, t):
        return quotient(self.parent * t - self.high - 1 + self.lift * self.coarse, self.coarse) - self.lift


def kernel(lx, ly, levels, off_x, off_y, nest, parent, nest_out, parent_out,
           fa, fb, pp, xs, xr, ys, yr, cs, cr, rs, rr, gx, gy, coarse, back,
           s_halo, r_halo, s_col, r_col, s_row, r_row, s_back, r_back):
    ix, iy = lax.axis_index("gx"), lax.axis_index("gy")
    ox, oy = off_x[0], off_y[0]
    cols, rows = lx.nest, ly.nest
    wide, high = fa.shape[3], fa.shape[2]
    fields = levels * 4
    n_before = lx.before[1] - lx.before[0] + 1
    n_after = lx.after[1] - lx.after[0] + 1
    n_col = max(n_before, n_after)

    def there(tx, ty):
        return {"gx": tx, "gy": ty}

    def send(ok, src, dst, ssem, rsem, tx, ty, local=True):
        mine = (tx == ix) & (ty == iy)

        @pl.when(ok & jnp.logical_not(mine))
        def _():
            pltpu.make_async_remote_copy(src, dst, ssem, rsem, device_id=there(tx, ty), device_id_type=MESH).start()

        if local:
            @pl.when(ok & mine)
            def _():
                pltpu.make_async_copy(src, dst, rsem).start()

    def sent(ok, src, ssem, tx, ty):
        @pl.when(ok & jnp.logical_not((tx == ix) & (ty == iy)))
        def _():
            pltpu.make_async_copy(src, src, ssem).wait()

    def arrived(ok, dst, rsem, blank=True):
        @pl.when(ok)
        def _():
            pltpu.make_async_copy(dst, dst, rsem).wait()

        if blank:
            @pl.when(jnp.logical_not(ok))
            def _():
                dst[...] = jnp.zeros(dst.shape, F32)

    lane = lax.broadcasted_iota(jnp.int32, (1, 128), 1)

    in_rows = (iy >= ly.tile_low) & (iy <= ly.tile_high)
    in_cols = (ix >= lx.tile_low) & (ix <= lx.tile_high)
    gives_west = (ix >= lx.before[0]) & (ix <= lx.before[1])
    gives_east = (ix >= lx.after[0]) & (ix <= lx.after[1])
    gives_col = in_rows & (gives_west | gives_east)
    col_to = jnp.where(gives_west, 0, lx.count - 1)
    col_slot = ix - jnp.where(gives_west, lx.before[0], lx.after[0])
    gives_south = iy == ly.before[0]
    gives_north = iy == ly.after[0]
    gives_row = in_cols & (gives_south | gives_north)
    row_to = jnp.where(gives_south, 0, ly.count - 1)

    @pl.when(gives_col)
    def _():
        want = ox + jnp.where(gives_west, -1, lx.span) - lx.parent * ix
        sub = lax.broadcasted_iota(jnp.int32, (lx.parent, ly.parent), 0)
        hit = sub == want

        def body(k, _):
            for c in range(4):
                line = jnp.sum(jnp.where(hit, parent[c, k], 0.0), axis=0, keepdims=True)
                cs[pl.ds(c * levels + k, 1), :] = line
            return 0

        lax.fori_loop(0, levels, body, 0)

    def col_targets():
        for j in range(ly.sources):
            ty = ly.base(iy) + j
            tyc = jnp.clip(ty, 0, ly.count - 1)
            ok = gives_col & (ty >= 0) & (ty < ly.count) & (iy >= ly.first(tyc)) & (iy <= ly.last(tyc))
            yield ok, j, tyc, jnp.clip(iy - ly.first(tyc), 0, ly.slots - 1)

    for ok, j, ty, part in col_targets():
        slot = jnp.clip(col_slot, 0, n_col - 1)
        send(ok, cs, cr.at[slot, part], s_col.at[j], r_col.at[slot, part], col_to, ty)

    @pl.when(gives_row)
    def _():
        want = oy + jnp.where(gives_south, -1, ly.span) - ly.parent * iy
        hit = lax.broadcasted_iota(jnp.int32, (lx.parent, ly.parent), 1) == want

        def body(k, acc):
            for c in range(4):
                line = jnp.sum(jnp.where(hit, parent[c, k], 0.0), axis=1, keepdims=True)
                acc = jnp.where(lane == c * levels + k, line, acc)
            return acc

        rs[...] = lax.fori_loop(0, levels, body, jnp.zeros((lx.parent, 128), F32))

    def row_targets():
        for j in range(lx.sources):
            tx = lx.base(ix) + j
            txc = jnp.clip(tx, 0, lx.count - 1)
            ok = gives_row & (tx >= 0) & (tx < lx.count) & (ix >= lx.first(txc)) & (ix <= lx.last(txc))
            yield ok, j, txc, jnp.clip(ix - lx.first(txc), 0, lx.slots - 1)

    for ok, j, tx, part in row_targets():
        send(ok, rs, rr.at[part], s_row.at[j], r_row.at[part], tx, row_to)

    half = levels // 2

    def pack_x(k, _):
        for c in range(4):
            for part in range(2):
                lev = k + part * half
                r = 4 * part
                xs[0, c, k, r:r + 3, :] = nest[c, lev, 0:3, :]
                xs[0, c, k, r + 3:r + 4, :] = parent[c, lev, 0:1, :]
                xs[1, c, k, r:r + 3, :] = nest[c, lev, cols - 3:cols, :]
                xs[1, c, k, r + 3:r + 4, :] = parent[c, lev, cols - 1:cols, :]
        return 0

    lax.fori_loop(0, half, pack_x, 0)

    has = {-1: lambda i, n: i > 0, 0: lambda i, n: i >= 0, 1: lambda i, n: i < n - 1}

    def neighbour(dx, dy):
        ok = has[dx](ix, lx.count) & has[dy](iy, ly.count)
        return ok, jnp.clip(ix + dx, 0, lx.count - 1), jnp.clip(iy + dy, 0, ly.count - 1)

    def halo_sends():
        for n, (dx, dy) in enumerate([(-1, 0), (1, 0), (0, -1), (0, 1), (-1, -1), (-1, 1), (1, -1), (1, 1)]):
            ok, tx, ty = neighbour(dx, dy)
            if dy == 0:
                src, dst = xs.at[(dx + 1) // 2], xr.at[(dx + 1) // 2]
            else:
                d = (dy + 1) // 2
                if dx == 0:
                    src, dst = ys.at[d], yr.at[d, pl.ds(0, cols)]
                elif dx < 0:
                    src, dst = ys.at[d, pl.ds(0, 8)], yr.at[d, pl.ds(cols, 8)]
                else:
                    src, dst = ys.at[d, pl.ds(cols - 8, 8)], yr.at[d, pl.ds(cols + 8, 8)]
            yield n, dx, dy, ok, tx, ty, src, dst

    for n, dx, dy, ok, tx, ty, src, dst in halo_sends():
        if dy == 0:
            send(ok, src, dst, s_halo.at[n], r_halo.at[n], tx, ty, local=False)

    def pack_y(k, acc):
        low, top = acc
        for c in range(4):
            at = 4 * (c * levels + k)
            mine = (lane >= at) & (lane < at + 4)
            a = jnp.where(lane < 3, nest[c, k, :, 0:128], pltpu.roll(parent[c, k, :, 0:128], 3, 1))
            b = jnp.where(lane < 3, pltpu.roll(nest[c, k, :, rows - 128:rows], 3, 1),
                          pltpu.roll(parent[c, k, :, rows - 128:rows], 4, 1))
            low = jnp.where(mine, pltpu.roll(a, at, 1), low)
            top = jnp.where(mine, pltpu.roll(b, at, 1), top)
        return low, top

    blank = jnp.zeros((cols, 128), F32)
    low, top = lax.fori_loop(0, levels, pack_y, (blank, blank))
    ys[0] = low
    ys[1] = top
    for n, dx, dy, ok, tx, ty, src, dst in halo_sends():
        if dy != 0:
            send(ok, src, dst, s_halo.at[n], r_halo.at[n], tx, ty, local=False)

    def middle(k, _):
        for c in range(4):
            fa[c, k, 0:cols, 0:rows] = nest[c, k]
            pp[c, k, 0:cols, 0:rows] = parent[c, k]
        return 0

    lax.fori_loop(0, levels, middle, 0)

    west, east = ix == 0, ix == lx.count - 1
    south, north = iy == 0, iy == ly.count - 1
    takes_col = west | east
    takes_row = south | north
    for s in range(n_col):
        live = (west & (s < n_before)) | (east & (s < n_after))
        for part in range(ly.slots):
            arrived(live & (ly.first(iy) + part <= ly.last(iy)), cr.at[s, part], r_col.at[s, part])
    for part in range(lx.slots):
        arrived(takes_row & (lx.first(ix) + part <= lx.last(ix)), rr.at[part], r_row.at[part])

    def third(v):
        return (((v + 3) * 21846) >> 16) - 1

    @pl.when(takes_col)
    def _():
        y = lax.broadcasted_iota(jnp.int32, (1, wide), 1)
        y = jnp.where(y < rows + 64, y, y - wide)
        place = oy + ly.coarse * iy - ly.parent * ly.first(iy) + third(y)
        total = jnp.zeros((fields, wide), F32)
        for part in range(ly.slots):
            k = lax.broadcasted_iota(jnp.int32, (ly.parent, wide), 0) + part * ly.parent
            table = jnp.where(k == place, 1.0, 0.0).astype(F32)
            strip = cr[0, part]
            for s in range(1, n_col):
                strip = strip + cr[s, part]
            total = total + jnp.dot(strip, table, precision=lax.Precision.HIGHEST, preferred_element_type=F32)
        for b in range(wide // 128):
            gx[b] = total[:, b * 128:b * 128 + 128]

    @pl.when(takes_row)
    def _():
        total = jnp.zeros((high, 128), F32)
        x = lax.broadcasted_iota(jnp.int32, (high, 1), 0)
        x = jnp.where(x < cols + 4, x, x - high)
        place = ox + lx.coarse * ix - lx.parent * lx.first(ix) + third(x)
        for part in range(lx.slots):
            k = lax.broadcasted_iota(jnp.int32, (high, lx.parent), 1) + part * lx.parent
            table = jnp.where(k == place, 1.0, 0.0).astype(F32)
            total = total + jnp.dot(table, rr[part], precision=lax.Precision.HIGHEST, preferred_element_type=F32)

        def body(k, _):
            for c in range(4):
                turned = pltpu.roll(total, lax.rem(128 - (c * levels + k), 128), 1)
                gy[c, k] = jnp.broadcast_to(turned[:, 0:1], (high, 128))
            return 0

        lax.fori_loop(0, levels, body, 0)

    sub8 = lax.broadcasted_iota(jnp.int32, (8, 1), 0)
    at_x = (sub8 == jnp.where(west, 7, -1)) | (sub8 == jnp.where(east, 0, -1))
    at_y = (lane == jnp.where(south, 127, -1)) | (lane == jnp.where(north, 0, -1))

    def put(dst, c, k, b, value):
        at = b * 128
        edge = jnp.where(at_x, gx[b, pl.ds(c * levels + k, 1), :], value[cols:high, :])
        inner = value[0:cols, :]
        if b == wide // 128 - 1:
            edge = jnp.where(at_y, gy[c, k, cols:high, :], edge)
            inner = jnp.where(at_y, gy[c, k, 0:cols, :], inner)
        dst[c, k, 0:cols, at:at + 128] = inner
        dst[c, k, cols:high, at:at + 128] = edge

    for n, dx, dy, ok, tx, ty, src, dst in halo_sends():
        back_ok, _, _ = neighbour(-dx, -dy)
        arrived(back_ok, dst, r_halo.at[n])

    def unpack(k, _):
        for c in range(4):
            for part in range(2):
                lev = k + part * half
                r = 4 * part
                fa[c, lev, cols:cols + 3, 0:rows] = xr[0, c, k, r:r + 3, :]
                pp[c, lev, cols:cols + 1, 0:rows] = xr[0, c, k, r + 3:r + 4, :]
                fa[c, lev, high - 3:high, 0:rows] = xr[1, c, k, r:r + 3, :]
                pp[c, lev, high - 1:high, 0:rows] = xr[1, c, k, r + 3:r + 4, :]
        return 0

    lax.fori_loop(0, half, unpack, 0)

    def side(d):
        corner = jnp.where(sub8 < 4, yr[d, cols:cols + 8, :], yr[d, cols + 8:cols + 16, :])
        return jnp.concatenate([yr[d, 0:cols, :], corner], axis=0)

    def unpack_y(k, both):
        after, before = both
        for c in range(4):
            at = 4 * (c * levels + k)
            a = pltpu.roll(after, lax.rem(128 - at, 128), 1)
            b = pltpu.roll(before, lax.rem(253 - at, 128), 1)
            block = jnp.where(lane < 64, a, b)
            fa[c, k, :, rows:wide] = jnp.where(at_y, gy[c, k], block)
            pp[c, k, :, rows:wide] = jnp.where(lane < 64, pltpu.roll(a, 125, 1), pltpu.roll(b, 127, 1))
            for m in range(wide // 128):
                here = slice(m * 128, m * 128 + 128)
                fa[c, k, cols:high, here] = jnp.where(at_x, gx[m, pl.ds(c * levels + k, 1), :], fa[c, k, cols:high, here])
        return both

    lax.fori_loop(0, levels, unpack_y, (side(0), side(1)))

    blocks, inner_blocks = wide // 128, rows // 128

    def advanced(src, k, b):
        at = slice(b * 128, b * 128 + 128)
        u, v, t, p = (src[c, k, :, at] for c in range(4))
        above = src[2, jnp.minimum(k + 1, levels - 1), :, at]
        below = src[2, jnp.maximum(k - 1, 0), :, at]
        after, before = (b + 1) % blocks * 128, (b - 1) % blocks * 128

        def dx(f):
            return pltpu.roll(f, high - 1, 0) - pltpu.roll(f, 1, 0)

        def dy(f):
            c, value = f
            ahead = jnp.where(lane == 0, src[c, k, :, after:after + 128], value)
            behind = jnp.where(lane == 127, src[c, k, :, before:before + 128], value)
            return pltpu.roll(ahead, 127, 1) - pltpu.roll(behind, 1, 1)

        ux, vy = dx(u), dy((1, v))
        hu, hv = u * (CARRY_RATE * 0.5), v * (CARRY_RATE * 0.5)
        s = SOUND_RATE * 0.5
        yield u - (hu * ux + hv * dy((0, u))) - s * dx(p)
        yield v - (hu * dx(v) + hv * vy) - s * dy((3, p))
        yield t - (hu * dx(t) + hv * dy((2, t))) + MIXING_RATE * (above - 2.0 * t + below)
        yield p - s * (ux + vy)

    for src, dst in ((fa, fb), (fb, fa)):
        def step(k, _, src=src, dst=dst):
            for b in range(blocks):
                for c, value in enumerate(advanced(src, k, b)):
                    put(dst, c, k, b, value)
            return 0

        lax.fori_loop(0, levels, step, 0)

    k = lax.broadcasted_iota(jnp.int32, (rows, ly.coarse), 0)
    j = lax.broadcasted_iota(jnp.int32, (rows, ly.coarse), 1)
    thirds = jnp.where((k >= 3 * j) & (k < 3 * j + 3), 1.0, 0.0).astype(F32)

    j = lax.broadcasted_iota(jnp.int32, (3 * lx.coarse, 3 * cols), 0)
    k = lax.broadcasted_iota(jnp.int32, (3 * lx.coarse, 3 * cols), 1)
    triples = jnp.where((k >= 3 * j) & (k < 3 * j + 3), 1.0, 0.0).astype(F32)

    def last_step(k):
        for b in range(inner_blocks):
            for c, value in enumerate(advanced(fa, k, b)):
                nest_out[c, k, :, b * 128:b * 128 + 128] = value[0:cols, :]
        inner = [nest_out[c, k] for c in range(3)]
        sums = jnp.dot(jnp.concatenate(inner, axis=0), thirds, precision=lax.Precision.HIGHEST,
                       preferred_element_type=F32)
        mean = jnp.dot(triples, sums, precision=lax.Precision.HIGHEST, preferred_element_type=F32) * (1.0 / 9.0)
        for c in range(3):
            coarse[k, c] = mean[c * lx.coarse:(c + 1) * lx.coarse, :]

    def back_targets():
        for a in range(lx.slots):
            for b in range(ly.slots):
                tx, ty = lx.first(ix) + a, ly.first(iy) + b
                ok = (tx <= lx.last(ix)) & (ty <= ly.last(iy))
                tx, ty = jnp.minimum(tx, lx.last(ix)), jnp.minimum(ty, ly.last(iy))
                yield ok, a, b, tx, ty, ix - lx.base(tx), iy - ly.base(ty)

    pair = 2

    def last_steps(q, _):
        for m in range(pair):
            last_step(q * pair + m)
        now = pl.ds(q * pair, pair)
        for ok, a, b, tx, ty, sx, sy in back_targets():
            send(ok, coarse.at[now], back.at[sx, sy, now], s_back.at[a, b, q], r_back.at[sx, sy, q], tx, ty)
        return 0

    lax.fori_loop(0, levels // pair, last_steps, 0)

    def parent_step(k, _):
        for b in range(inner_blocks):
            for c, value in enumerate(advanced(pp, k, b)):
                parent_out[c, k, :, b * 128:b * 128 + 128] = value[0:lx.parent, :]
        return 0

    lax.fori_loop(0, levels, parent_step, 0)

    takes_back = in_rows & in_cols

    @pl.when(takes_back)
    def _():
        col = lax.broadcasted_iota(jnp.int32, (lx.parent, ly.parent), 0) + lx.parent * ix - ox
        row = lax.broadcasted_iota(jnp.int32, (lx.parent, ly.parent), 1) + ly.parent * iy - oy
        inside = (col >= 0) & (col < lx.span) & (row >= 0) & (row < ly.span)
        x0 = lx.parent * ix - lx.coarse * lx.base(ix) - ox
        y0 = ly.parent * iy - ly.coarse * ly.base(iy) - oy
        nsx, nsy = lx.window // lx.coarse, ly.window // ly.coarse

        def body(q, _):
            now = pl.ds(q * pair, pair)
            for a in range(lx.sources):
                for b in range(ly.sources):
                    sx, sy = lx.base(ix) + a, ly.base(iy) + b
                    sxc, syc = jnp.clip(sx, 0, lx.count - 1), jnp.clip(sy, 0, ly.count - 1)
                    ok = (sx == sxc) & (sy == syc)
                    ok = ok & (ix >= lx.first(sxc)) & (ix <= lx.last(sxc))
                    ok = ok & (iy >= ly.first(syc)) & (iy <= ly.last(syc))
                    arrived(ok, back.at[a, b, now], r_back.at[a, b, q], blank=False)
            for m in range(pair):
                k = q * pair + m
                for c in range(3):
                    whole = jnp.concatenate(
                        [jnp.concatenate([back[a, b, k, c] for b in range(nsy)], axis=1) for a in range(nsx)],
                        axis=0)
                    moved = pltpu.roll(whole, lx.window - x0, 0)[0:lx.parent, :]
                    moved = pltpu.roll(moved, ly.window - y0, 1)
                    parent_out[c, k] = jnp.where(inside, moved[:, 0:ly.parent], parent_out[c, k])
            return 0

        lax.fori_loop(0, levels // pair, body, 0)

    for ok, j, ty, part in col_targets():
        sent(ok, cs, s_col.at[j], col_to, ty)
    for ok, j, tx, part in row_targets():
        sent(ok, rs, s_row.at[j], tx, row_to)
    for n, dx, dy, ok, tx, ty, src, dst in halo_sends():
        sent(ok, src, s_halo.at[n], tx, ty)
    for q in range(levels // pair):
        now = pl.ds(q * pair, pair)
        for ok, a, b, tx, ty, sx, sy in back_targets():
            sent(ok, coarse.at[now], s_back.at[a, b, q], tx, ty)


def on_device(lx, ly, nest_state, parent_state, offset_x, offset_y):
    levels = nest_state.shape[1]
    cols, rows = nest_state.shape[2:]
    high, wide = cols + 8, rows + 128
    n_col = max(lx.before[1] - lx.before[0], lx.after[1] - lx.after[0]) + 1
    padded = pltpu.VMEM((4, levels, high, wide), F32)
    dma = pltpu.SemaphoreType.DMA
    nbx, nby = lx.window // lx.coarse, ly.window // ly.coarse
    vm = pl.BlockSpec(memory_space=pltpu.VMEM)
    sm = pl.BlockSpec(memory_space=pltpu.SMEM)
    shape = jax.ShapeDtypeStruct(nest_state.shape, F32)
    return pl.pallas_call(
        functools.partial(kernel, lx, ly, levels),
        out_shape=(shape, shape),
        in_specs=[sm, sm, vm, vm],
        out_specs=(vm, vm),
        scratch_shapes=[
            padded, padded, padded,
            pltpu.VMEM((2, 4, levels // 2, 8, rows), F32),
            pltpu.VMEM((2, 4, levels // 2, 8, rows), F32),
            pltpu.VMEM((2, cols, 128), F32),
            pltpu.VMEM((2, cols + 16, 128), F32),
            pltpu.VMEM((4 * levels, ly.parent), F32),
            pltpu.VMEM((n_col, ly.slots, 4 * levels, ly.parent), F32),
            pltpu.VMEM((lx.parent, 128), F32),
            pltpu.VMEM((lx.slots, lx.parent, 128), F32),
            pltpu.VMEM((wide // 128, 4 * levels, 128), F32),
            pltpu.VMEM((4, levels, high, 128), F32),
            pltpu.VMEM((levels, 3, lx.coarse, ly.coarse), F32),
            pltpu.VMEM((nbx, nby, levels, 3, lx.coarse, ly.coarse), F32),
            dma((8,)), dma((8,)),
            dma((ly.sources,)), dma((n_col, ly.slots)),
            dma((lx.sources,)), dma((lx.slots,)),
            dma((lx.slots, ly.slots, levels // 2)), dma((nbx, nby, levels // 2)),
        ],
        compiler_params=pltpu.CompilerParams(has_side_effects=True, vmem_limit_bytes=48 * 1024 * 1024),
    )(offset_x, offset_y, nest_state, parent_state)


def solution(mesh):
    placed = (P(None, None, "gx", "gy"), P(None, None, "gx", "gy"), P(), P())
    count_x, count_y = mesh.shape["gx"], mesh.shape["gy"]

    def program(nest_state, parent_state, offset_x, offset_y):
        lx = Line(count_x, parent_state.shape[2] // count_x, nest_state.shape[2] // count_x, 1)
        rows = parent_state.shape[3] // count_y
        ly = Line(count_y, rows, nest_state.shape[3] // count_y, rows + 1)
        return jax.shard_map(
            functools.partial(on_device, lx, ly),
            mesh=mesh,
            in_specs=placed,
            out_specs=(P(None, None, "gx", "gy"), P(None, None, "gx", "gy")),
            check_vma=False,
        )(nest_state, parent_state, offset_x, offset_y)

    return program
```

```python
import functools

import jax
import jax.numpy as jnp
from jax import lax
from jax.experimental import pallas as pl
from jax.experimental.pallas import tpu as pltpu
from jax.sharding import PartitionSpec as P

SUBSTEPS = 3
CARRY_RATE = 0.35
SOUND_RATE = 0.4
MIXING_RATE = 0.2
MESH = pl.DeviceIdType.MESH
F32 = jnp.float32


def quotient(a, b):
    return a // b if isinstance(a, int) else lax.div(a, jnp.int32(b))


class Line:
    def __init__(self, count, parent, nest, lowest):
        self.count, self.parent, self.nest = count, parent, nest
        self.coarse = nest // 3
        span = count * self.coarse
        self.span = span
        self.low = max(lowest, (count // 2 - 1) * parent - span)
        self.high = max(self.low, min(count * parent - span, (count // 2) * parent - span) - 1)
        self.lift = self.high // self.coarse + 2
        tiles = range(count)
        self.slots = max(self.last(i) - self.first(i) + 1 for i in tiles)
        hit = [(t, i) for i in tiles for t in range(self.first(i), self.last(i) + 1)]
        assert all(0 <= t < count for t, _ in hit)
        self.sources = max(i - self.base(t) + 1 for t, i in hit)
        assert min(i - self.base(t) for t, i in hit) >= 0
        reach = max(parent * t - self.coarse * self.base(t) - self.low for t, _ in hit) + parent
        self.window = max(self.sources, -(-reach // self.coarse)) * self.coarse
        self.tile_low, self.tile_high = self.first(0), self.last(count - 1)
        self.before = ((self.low - 1) // parent, (self.high - 1) // parent)
        self.after = ((self.low + span) // parent, (self.high + span) // parent)
        assert self.before[1] < self.after[0]

    def first(self, i):
        return quotient(self.low + self.coarse * i - 1, self.parent)

    def last(self, i):
        return quotient(self.high + self.coarse * i + self.coarse, self.parent)

    def base(self, t):
        return quotient(self.parent * t - self.high - 1 + self.lift * self.coarse, self.coarse) - self.lift


def kernel(lx, ly, levels, off_x, off_y, nest, parent, nest_out, parent_out,
           fa, fb, pp, xs, xr, ys, yr, cs, cr, rs, rr, gx, gy, coarse, back,
           s_halo, r_halo, s_col, r_col, s_row, r_row, s_back, r_back):
    ix, iy = lax.axis_index("gx"), lax.axis_index("gy")
    ox, oy = off_x[0], off_y[0]
    cols, rows = lx.nest, ly.nest
    wide, high = fa.shape[3], fa.shape[2]
    fields = levels * 4
    n_before = lx.before[1] - lx.before[0] + 1
    n_after = lx.after[1] - lx.after[0] + 1
    n_col = max(n_before, n_after)

    def there(tx, ty):
        return {"gx": tx, "gy": ty}

    def send(ok, src, dst, ssem, rsem, tx, ty, local=True):
        mine = (tx == ix) & (ty == iy)

        @pl.when(ok & jnp.logical_not(mine))
        def _():
            pltpu.make_async_remote_copy(src, dst, ssem, rsem, device_id=there(tx, ty), device_id_type=MESH).start()

        if local:
            @pl.when(ok & mine)
            def _():
                pltpu.make_async_copy(src, dst, rsem).start()

    def sent(ok, src, ssem, tx, ty):
        @pl.when(ok & jnp.logical_not((tx == ix) & (ty == iy)))
        def _():
            pltpu.make_async_copy(src, src, ssem).wait()

    def arrived(ok, dst, rsem, blank=True):
        @pl.when(ok)
        def _():
            pltpu.make_async_copy(dst, dst, rsem).wait()

        if blank:
            @pl.when(jnp.logical_not(ok))
            def _():
                dst[...] = jnp.zeros(dst.shape, F32)

    lane = lax.broadcasted_iota(jnp.int32, (1, 128), 1)

    in_rows = (iy >= ly.tile_low) & (iy <= ly.tile_high)
    in_cols = (ix >= lx.tile_low) & (ix <= lx.tile_high)
    gives_west = (ix >= lx.before[0]) & (ix <= lx.before[1])
    gives_east = (ix >= lx.after[0]) & (ix <= lx.after[1])
    gives_col = in_rows & (gives_west | gives_east)
    col_to = jnp.where(gives_west, 0, lx.count - 1)
    col_slot = ix - jnp.where(gives_west, lx.before[0], lx.after[0])
    gives_south = iy == ly.before[0]
    gives_north = iy == ly.after[0]
    gives_row = in_cols & (gives_south | gives_north)
    row_to = jnp.where(gives_south, 0, ly.count - 1)

    def col_targets():
        for j in range(ly.sources):
            ty = ly.base(iy) + j
            tyc = jnp.clip(ty, 0, ly.count - 1)
            ok = gives_col & (ty >= 0) & (ty < ly.count) & (iy >= ly.first(tyc)) & (iy <= ly.last(tyc))
            yield ok, j, tyc, jnp.clip(iy - ly.first(tyc), 0, ly.slots - 1)

    def row_targets():
        for j in range(lx.sources):
            tx = lx.base(ix) + j
            txc = jnp.clip(tx, 0, lx.count - 1)
            ok = gives_row & (tx >= 0) & (tx < lx.count) & (ix >= lx.first(txc)) & (ix <= lx.last(txc))
            yield ok, j, txc, jnp.clip(ix - lx.first(txc), 0, lx.slots - 1)

    has = {-1: lambda i, n: i > 0, 0: lambda i, n: i >= 0, 1: lambda i, n: i < n - 1}

    def neighbour(dx, dy):
        ok = has[dx](ix, lx.count) & has[dy](iy, ly.count)
        return ok, jnp.clip(ix + dx, 0, lx.count - 1), jnp.clip(iy + dy, 0, ly.count - 1)

    def halo_sends():
        for n, (dx, dy) in enumerate([(-1, 0), (1, 0), (0, -1), (0, 1), (-1, -1), (-1, 1), (1, -1), (1, 1)]):
            ok, tx, ty = neighbour(dx, dy)
            if dy == 0:
                src, dst = xs.at[(dx + 1) // 2], xr.at[(dx + 1) // 2]
            else:
                d = (dy + 1) // 2
                if dx == 0:
                    src, dst = ys.at[d], yr.at[d, pl.ds(0, cols)]
                elif dx < 0:
                    src, dst = ys.at[d, pl.ds(0, 8)], yr.at[d, pl.ds(cols, 8)]
                else:
                    src, dst = ys.at[d, pl.ds(cols - 8, 8)], yr.at[d, pl.ds(cols + 8, 8)]
            yield n, dx, dy, ok, tx, ty, src, dst

    def back_targets():
        for a in range(lx.slots):
            for b in range(ly.slots):
                tx, ty = lx.first(ix) + a, ly.first(iy) + b
                ok = (tx <= lx.last(ix)) & (ty <= ly.last(iy))
                tx, ty = jnp.minimum(tx, lx.last(ix)), jnp.minimum(ty, ly.last(iy))
                yield ok, a, b, tx, ty, ix - lx.base(tx), iy - ly.base(ty)

    takes_back = in_rows & in_cols
    west, east = ix == 0, ix == lx.count - 1
    south, north = iy == 0, iy == ly.count - 1
    takes_col = west | east
    takes_row = south | north

    def col_slots():
        for s in range(n_col):
            live = (west & (s < n_before)) | (east & (s < n_after))
            tx = jnp.where(west, lx.before[0] + s, lx.after[0] + s)
            for part in range(ly.slots):
                ok = live & (ly.first(iy) + part <= ly.last(iy))
                yield ok, s, part, jnp.minimum(tx, lx.count - 1), jnp.minimum(ly.first(iy) + part, ly.last(iy))

    def row_slots():
        for part in range(lx.slots):
            ok = takes_row & (lx.first(ix) + part <= lx.last(ix))
            yield ok, part, jnp.minimum(lx.first(ix) + part, lx.last(ix)), jnp.where(south, ly.before[0], ly.after[0])

    def back_slots():
        for a in range(lx.sources):
            for b in range(ly.sources):
                sx, sy = lx.base(ix) + a, ly.base(iy) + b
                sxc, syc = jnp.clip(sx, 0, lx.count - 1), jnp.clip(sy, 0, ly.count - 1)
                ok = takes_back & (sx == sxc) & (sy == syc)
                ok = ok & (ix >= lx.first(sxc)) & (ix <= lx.last(sxc))
                ok = ok & (iy >= ly.first(syc)) & (iy <= ly.last(syc))
                yield ok, a, b, sxc, syc

    barrier = pltpu.get_barrier_semaphore()

    def greet(ok, tx, ty):
        @pl.when(ok & jnp.logical_not((tx == ix) & (ty == iy)))
        def _():
            pl.semaphore_signal(barrier, inc=1, device_id=there(tx, ty), device_id_type=MESH)

    expected = jnp.int32(0)

    def count(ok, tx, ty):
        return jnp.where(ok & jnp.logical_not((tx == ix) & (ty == iy)), 1, 0).astype(jnp.int32)

    for n, dx, dy, ok, tx, ty, src, dst in halo_sends():
        greet(ok, tx, ty)
        expected = expected + count(ok, tx, ty)
    for ok, s, part, tx, ty in col_slots():
        greet(ok, tx, ty)
    for ok, part, tx, ty in row_slots():
        greet(ok, tx, ty)
    for ok, a, b, tx, ty in back_slots():
        greet(ok, tx, ty)
    for ok, j, ty, part in col_targets():
        expected = expected + count(ok, col_to, ty)
    for ok, j, tx, part in row_targets():
        expected = expected + count(ok, tx, row_to)
    for ok, a, b, tx, ty, sx, sy in back_targets():
        expected = expected + count(ok, tx, ty)

    half = levels // 2

    def pack_x(k, _):
        for c in range(4):
            for part in range(2):
                lev = k + part * half
                r = 4 * part
                xs[0, c, k, r:r + 3, :] = nest[c, lev, 0:3, :]
                xs[0, c, k, r + 3:r + 4, :] = parent[c, lev, 0:1, :]
                xs[1, c, k, r:r + 3, :] = nest[c, lev, cols - 3:cols, :]
                xs[1, c, k, r + 3:r + 4, :] = parent[c, lev, cols - 1:cols, :]
        return 0

    lax.fori_loop(0, half, pack_x, 0)

    def pack_y(k, acc):
        low, top = acc
        for c in range(4):
            at = 4 * (c * levels + k)
            mine = (lane >= at) & (lane < at + 4)
            a = jnp.where(lane < 3, nest[c, k, :, 0:128], pltpu.roll(parent[c, k, :, 0:128], 3, 1))
            b = jnp.where(lane < 3, pltpu.roll(nest[c, k, :, rows - 128:rows], 3, 1),
                          pltpu.roll(parent[c, k, :, rows - 128:rows], 4, 1))
            low = jnp.where(mine, pltpu.roll(a, at, 1), low)
            top = jnp.where(mine, pltpu.roll(b, at, 1), top)
        return low, top

    blank = jnp.zeros((cols, 128), F32)
    low, top = lax.fori_loop(0, levels, pack_y, (blank, blank))
    ys[0] = low
    ys[1] = top
    pl.semaphore_wait(barrier, expected)
    for n, dx, dy, ok, tx, ty, src, dst in halo_sends():
        send(ok, src, dst, s_halo.at[n], r_halo.at[n], tx, ty, local=False)

    @pl.when(gives_col)
    def _():
        want = ox + jnp.where(gives_west, -1, lx.span) - lx.parent * ix
        sub = lax.broadcasted_iota(jnp.int32, (lx.parent, ly.parent), 0)
        hit = sub == want

        def body(k, _):
            for c in range(4):
                line = jnp.sum(jnp.where(hit, parent[c, k], 0.0), axis=0, keepdims=True)
                cs[pl.ds(c * levels + k, 1), :] = line
            return 0

        lax.fori_loop(0, levels, body, 0)

    for ok, j, ty, part in col_targets():
        slot = jnp.clip(col_slot, 0, n_col - 1)
        send(ok, cs, cr.at[slot, part], s_col.at[j], r_col.at[slot, part], col_to, ty)

    @pl.when(gives_row)
    def _():
        want = oy + jnp.where(gives_south, -1, ly.span) - ly.parent * iy
        hit = lax.broadcasted_iota(jnp.int32, (lx.parent, ly.parent), 1) == want

        def body(k, acc):
            for c in range(4):
                line = jnp.sum(jnp.where(hit, parent[c, k], 0.0), axis=1, keepdims=True)
                acc = jnp.where(lane == c * levels + k, line, acc)
            return acc

        rs[...] = lax.fori_loop(0, levels, body, jnp.zeros((lx.parent, 128), F32))

    for ok, j, tx, part in row_targets():
        send(ok, rs, rr.at[part], s_row.at[j], r_row.at[part], tx, row_to)

    def middle(k, _):
        for c in range(4):
            fa[c, k, 0:cols, 0:rows] = nest[c, k]
            pp[c, k, 0:cols, 0:rows] = parent[c, k]
        return 0

    lax.fori_loop(0, levels, middle, 0)

    for ok, s, part, tx, ty in col_slots():
        arrived(ok, cr.at[s, part], r_col.at[s, part])
    for ok, part, tx, ty in row_slots():
        arrived(ok, rr.at[part], r_row.at[part])

    def third(v):
        return (((v + 3) * 21846) >> 16) - 1

    @pl.when(takes_col)
    def _():
        y = lax.broadcasted_iota(jnp.int32, (1, wide), 1)
        y = jnp.where(y < rows + 64, y, y - wide)
        place = oy + ly.coarse * iy - ly.parent * ly.first(iy) + third(y)
        total = jnp.zeros((fields, wide), F32)
        for part in range(ly.slots):
            k = lax.broadcasted_iota(jnp.int32, (ly.parent, wide), 0) + part * ly.parent
            table = jnp.where(k == place, 1.0, 0.0).astype(F32)
            strip = cr[0, part]
            for s in range(1, n_col):
                strip = strip + cr[s, part]
            total = total + jnp.dot(strip, table, precision=lax.Precision.HIGHEST, preferred_element_type=F32)
        for b in range(wide // 128):
            gx[b] = total[:, b * 128:b * 128 + 128]

    @pl.when(takes_row)
    def _():
        total = jnp.zeros((high, 128), F32)
        x = lax.broadcasted_iota(jnp.int32, (high, 1), 0)
        x = jnp.where(x < cols + 4, x, x - high)
        place = ox + lx.coarse * ix - lx.parent * lx.first(ix) + third(x)
        for part in range(lx.slots):
            k = lax.broadcasted_iota(jnp.int32, (high, lx.parent), 1) + part * lx.parent
            table = jnp.where(k == place, 1.0, 0.0).astype(F32)
            total = total + jnp.dot(table, rr[part], precision=lax.Precision.HIGHEST, preferred_element_type=F32)

        def body(k, _):
            for c in range(4):
                turned = pltpu.roll(total, lax.rem(128 - (c * levels + k), 128), 1)
                gy[c, k] = jnp.broadcast_to(turned[:, 0:1], (high, 128))
            return 0

        lax.fori_loop(0, levels, body, 0)

    sub8 = lax.broadcasted_iota(jnp.int32, (8, 1), 0)
    at_x = (sub8 == jnp.where(west, 7, -1)) | (sub8 == jnp.where(east, 0, -1))
    at_y = (lane == jnp.where(south, 127, -1)) | (lane == jnp.where(north, 0, -1))

    def put(dst, c, k, b, value):
        at = b * 128
        edge = jnp.where(at_x, gx[b, pl.ds(c * levels + k, 1), :], value[cols:high, :])
        inner = value[0:cols, :]
        if b == wide // 128 - 1:
            edge = jnp.where(at_y, gy[c, k, cols:high, :], edge)
            inner = jnp.where(at_y, gy[c, k, 0:cols, :], inner)
        dst[c, k, 0:cols, at:at + 128] = inner
        dst[c, k, cols:high, at:at + 128] = edge

    for n, dx, dy, ok, tx, ty, src, dst in halo_sends():
        back_ok, _, _ = neighbour(-dx, -dy)
        arrived(back_ok, dst, r_halo.at[n])

    def unpack(k, _):
        for c in range(4):
            for part in range(2):
                lev = k + part * half
                r = 4 * part
                fa[c, lev, cols:cols + 3, 0:rows] = xr[0, c, k, r:r + 3, :]
                pp[c, lev, cols:cols + 1, 0:rows] = xr[0, c, k, r + 3:r + 4, :]
                fa[c, lev, high - 3:high, 0:rows] = xr[1, c, k, r:r + 3, :]
                pp[c, lev, high - 1:high, 0:rows] = xr[1, c, k, r + 3:r + 4, :]
        return 0

    lax.fori_loop(0, half, unpack, 0)

    def side(d):
        corner = jnp.where(sub8 < 4, yr[d, cols:cols + 8, :], yr[d, cols + 8:cols + 16, :])
        return jnp.concatenate([yr[d, 0:cols, :], corner], axis=0)

    def unpack_y(k, both):
        after, before = both
        for c in range(4):
            at = 4 * (c * levels + k)
            a = pltpu.roll(after, lax.rem(128 - at, 128), 1)
            b = pltpu.roll(before, lax.rem(253 - at, 128), 1)
            block = jnp.where(lane < 64, a, b)
            fa[c, k, :, rows:wide] = jnp.where(at_y, gy[c, k], block)
            pp[c, k, :, rows:wide] = jnp.where(lane < 64, pltpu.roll(a, 125, 1), pltpu.roll(b, 127, 1))
            for m in range(wide // 128):
                here = slice(m * 128, m * 128 + 128)
                fa[c, k, cols:high, here] = jnp.where(at_x, gx[m, pl.ds(c * levels + k, 1), :], fa[c, k, cols:high, here])
        return both

    lax.fori_loop(0, levels, unpack_y, (side(0), side(1)))

    blocks, inner_blocks = wide // 128, rows // 128

    def advanced(src, k, b):
        at = slice(b * 128, b * 128 + 128)
        u, v, t, p = (src[c, k, :, at] for c in range(4))
        above = src[2, jnp.minimum(k + 1, levels - 1), :, at]
        below = src[2, jnp.maximum(k - 1, 0), :, at]
        after, before = (b + 1) % blocks * 128, (b - 1) % blocks * 128

        def dx(f):
            return pltpu.roll(f, high - 1, 0) - pltpu.roll(f, 1, 0)

        def dy(f):
            c, value = f
            ahead = jnp.where(lane == 0, src[c, k, :, after:after + 128], value)
            behind = jnp.where(lane == 127, src[c, k, :, before:before + 128], value)
            return pltpu.roll(ahead, 127, 1) - pltpu.roll(behind, 1, 1)

        ux, vy = dx(u), dy((1, v))
        hu, hv = u * (CARRY_RATE * 0.5), v * (CARRY_RATE * 0.5)
        s = SOUND_RATE * 0.5
        yield u - (hu * ux + hv * dy((0, u))) - s * dx(p)
        yield v - (hu * dx(v) + hv * vy) - s * dy((3, p))
        yield t - (hu * dx(t) + hv * dy((2, t))) + MIXING_RATE * (above - 2.0 * t + below)
        yield p - s * (ux + vy)

    for src, dst in ((fa, fb), (fb, fa)):
        def step(k, _, src=src, dst=dst):
            for b in range(blocks):
                for c, value in enumerate(advanced(src, k, b)):
                    put(dst, c, k, b, value)
            return 0

        lax.fori_loop(0, levels, step, 0)

    k = lax.broadcasted_iota(jnp.int32, (rows, ly.coarse), 0)
    j = lax.broadcasted_iota(jnp.int32, (rows, ly.coarse), 1)
    thirds = jnp.where((k >= 3 * j) & (k < 3 * j + 3), 1.0, 0.0).astype(F32)

    j = lax.broadcasted_iota(jnp.int32, (3 * lx.coarse, 3 * cols), 0)
    k = lax.broadcasted_iota(jnp.int32, (3 * lx.coarse, 3 * cols), 1)
    triples = jnp.where((k >= 3 * j) & (k < 3 * j + 3), 1.0, 0.0).astype(F32)

    def last_step(k):
        for b in range(inner_blocks):
            for c, value in enumerate(advanced(fa, k, b)):
                nest_out[c, k, :, b * 128:b * 128 + 128] = value[0:cols, :]
        inner = [nest_out[c, k] for c in range(3)]
        sums = jnp.dot(jnp.concatenate(inner, axis=0), thirds, precision=lax.Precision.HIGHEST,
                       preferred_element_type=F32)
        mean = jnp.dot(triples, sums, precision=lax.Precision.HIGHEST, preferred_element_type=F32) * (1.0 / 9.0)
        for c in range(3):
            coarse[k, c] = mean[c * lx.coarse:(c + 1) * lx.coarse, :]

    pair = 2

    def last_steps(q, _):
        for m in range(pair):
            last_step(q * pair + m)
        now = pl.ds(q * pair, pair)
        for ok, a, b, tx, ty, sx, sy in back_targets():
            send(ok, coarse.at[now], back.at[sx, sy, now], s_back.at[a, b, q], r_back.at[sx, sy, q], tx, ty)
        return 0

    lax.fori_loop(0, levels // pair, last_steps, 0)

    def parent_step(k, _):
        for b in range(inner_blocks):
            for c, value in enumerate(advanced(pp, k, b)):
                parent_out[c, k, :, b * 128:b * 128 + 128] = value[0:lx.parent, :]
        return 0

    lax.fori_loop(0, levels, parent_step, 0)

    @pl.when(takes_back)
    def _():
        col = lax.broadcasted_iota(jnp.int32, (lx.parent, ly.parent), 0) + lx.parent * ix - ox
        row = lax.broadcasted_iota(jnp.int32, (lx.parent, ly.parent), 1) + ly.parent * iy - oy
        inside = (col >= 0) & (col < lx.span) & (row >= 0) & (row < ly.span)
        x0 = lx.parent * ix - lx.coarse * lx.base(ix) - ox
        y0 = ly.parent * iy - ly.coarse * ly.base(iy) - oy
        nsx, nsy = lx.window // lx.coarse, ly.window // ly.coarse

        def body(q, _):
            now = pl.ds(q * pair, pair)
            for ok, a, b, sx, sy in back_slots():
                arrived(ok, back.at[a, b, now], r_back.at[a, b, q], blank=False)
            for m in range(pair):
                k = q * pair + m
                for c in range(3):
                    whole = jnp.concatenate(
                        [jnp.concatenate([back[a, b, k, c] for b in range(nsy)], axis=1) for a in range(nsx)],
                        axis=0)
                    moved = pltpu.roll(whole, lx.window - x0, 0)[0:lx.parent, :]
                    moved = pltpu.roll(moved, ly.window - y0, 1)
                    parent_out[c, k] = jnp.where(inside, moved[:, 0:ly.parent], parent_out[c, k])
            return 0

        lax.fori_loop(0, levels // pair, body, 0)

    for ok, j, ty, part in col_targets():
        sent(ok, cs, s_col.at[j], col_to, ty)
    for ok, j, tx, part in row_targets():
        sent(ok, rs, s_row.at[j], tx, row_to)
    for n, dx, dy, ok, tx, ty, src, dst in halo_sends():
        sent(ok, src, s_halo.at[n], tx, ty)
    for q in range(levels // pair):
        now = pl.ds(q * pair, pair)
        for ok, a, b, tx, ty, sx, sy in back_targets():
            sent(ok, coarse.at[now], s_back.at[a, b, q], tx, ty)


def on_device(lx, ly, nest_state, parent_state, offset_x, offset_y):
    levels = nest_state.shape[1]
    cols, rows = nest_state.shape[2:]
    high, wide = cols + 8, rows + 128
    n_col = max(lx.before[1] - lx.before[0], lx.after[1] - lx.after[0]) + 1
    padded = pltpu.VMEM((4, levels, high, wide), F32)
    dma = pltpu.SemaphoreType.DMA
    nbx, nby = lx.window // lx.coarse, ly.window // ly.coarse
    vm = pl.BlockSpec(memory_space=pltpu.VMEM)
    sm = pl.BlockSpec(memory_space=pltpu.SMEM)
    shape = jax.ShapeDtypeStruct(nest_state.shape, F32)
    return pl.pallas_call(
        functools.partial(kernel, lx, ly, levels),
        out_shape=(shape, shape),
        in_specs=[sm, sm, vm, vm],
        out_specs=(vm, vm),
        scratch_shapes=[
            padded, padded, padded,
            pltpu.VMEM((2, 4, levels // 2, 8, rows), F32),
            pltpu.VMEM((2, 4, levels // 2, 8, rows), F32),
            pltpu.VMEM((2, cols, 128), F32),
            pltpu.VMEM((2, cols + 16, 128), F32),
            pltpu.VMEM((4 * levels, ly.parent), F32),
            pltpu.VMEM((n_col, ly.slots, 4 * levels, ly.parent), F32),
            pltpu.VMEM((lx.parent, 128), F32),
            pltpu.VMEM((lx.slots, lx.parent, 128), F32),
            pltpu.VMEM((wide // 128, 4 * levels, 128), F32),
            pltpu.VMEM((4, levels, high, 128), F32),
            pltpu.VMEM((levels, 3, lx.coarse, ly.coarse), F32),
            pltpu.VMEM((nbx, nby, levels, 3, lx.coarse, ly.coarse), F32),
            dma((8,)), dma((8,)),
            dma((ly.sources,)), dma((n_col, ly.slots)),
            dma((lx.sources,)), dma((lx.slots,)),
            dma((lx.slots, ly.slots, levels // 2)), dma((nbx, nby, levels // 2)),
        ],
        compiler_params=pltpu.CompilerParams(collective_id=0, has_side_effects=True, vmem_limit_bytes=48 * 1024 * 1024),
    )(offset_x, offset_y, nest_state, parent_state)


def solution(mesh):
    placed = (P(None, None, "gx", "gy"), P(None, None, "gx", "gy"), P(), P())
    count_x, count_y = mesh.shape["gx"], mesh.shape["gy"]

    def program(nest_state, parent_state, offset_x, offset_y):
        lx = Line(count_x, parent_state.shape[2] // count_x, nest_state.shape[2] // count_x, 1)
        rows = parent_state.shape[3] // count_y
        ly = Line(count_y, rows, nest_state.shape[3] // count_y, rows + 1)
        return jax.shard_map(
            functools.partial(on_device, lx, ly),
            mesh=mesh,
            in_specs=placed,
            out_specs=(P(None, None, "gx", "gy"), P(None, None, "gx", "gy")),
            check_vma=False,
        )(nest_state, parent_state, offset_x, offset_y)

    return program
```
